256 devices in a mesh: trow: 8 (over z_lo, core), tcol: 32 (over z_hi, y, x).
Axes of the slice: x: 4, y: 4, z: 8 (z_hi: 2, z_lo: 4; z = z_hi * 4 + z_lo), core: 2. Of those that a mesh axis runs over, the one named last changes fastest.
Arguments:
- hist_lesser: float32 [8, 32, 9, 2, 256, 256], P('trow', 'tcol'), may hold values from -6 to 6
- self_greater: float32 [64, 2, 256, 256], P('tcol'), may hold values from -0.046875 to 0.046875
- self_lesser: float32 [64, 2, 256, 256], P('tcol'), may hold values from -0.046875 to 0.046875
- row_old: float32 [32, 2, 2, 256, 256], P('tcol', None, None, 'trow'), may hold values from -6 to 6
- hopping: float32 [2, 256, 256], replicated, may hold values from -0.375 to 0.375
- damping: float32 [256], replicated, may hold values from 0.2 to 2
Outputs:
- row_new: float32 [32, 2, 2, 256, 256], P('tcol', None, None, 'trow')
- sigma_hop: float32 [32, 2, 2, 256, 256], P('tcol', None, None, 'trow')
The draws below stay inside these ranges and needn't reach their ends.
All inputs are finite; a program needn't handle non-finite values.
Results may differ from the reference program's by a relative error of at most 0.0003.
Values sent between devices are 32-bit elements; how exact they have to be, the bound alone decides.
A program may use at most 128 MiB of HBM per device.

```python
import math
import jax
import jax.numpy as jnp
from jax import lax

SITES = 256
PAIRS = 32
WINDOW = 64
HALF_BLOCK = 4
SLOTS = 9
N_TROW = 8


def block_levels(rng, dims, pieces, least, top_value):
    def one(axis_at, parts):
        heights = jax.random.uniform(jax.random.fold_in(jax.random.fold_in(rng, 6), axis_at), (parts,), jnp.float32, least / len(pieces), top_value / len(pieces))
        return jnp.repeat(jnp.exp(heights), dims[axis_at] // parts).reshape((-1,) + (1,) * (len(dims) - axis_at - 1))

    factor_of = one(*pieces[0])
    for cut in pieces[1:]:
        factor_of = factor_of * one(*cut)
    return factor_of


def centred(rng, dims, deviation, limit, split=(), held_as=jnp.bfloat16):
    loudness = block_levels(rng, dims, split, -0.22, 0.18) if split else 1.0
    array = jax.random.normal(rng, dims, jnp.float32) * deviation * loudness
    return jnp.minimum(jnp.maximum(array, -limit), limit).astype(held_as)


def setup_inputs(seed: int = 0) -> dict:
    key_list = jax.random.split(jax.random.key(seed), 7)
    return {
        "hist_lesser": centred(key_list[0], (N_TROW, PAIRS, SLOTS, 2, SITES, SITES), 1.0, 6.0, ((0, 8), (1, 32)), jnp.float32),
        "self_greater": centred(key_list[1], (WINDOW, 2, SITES, SITES), (SITES * WINDOW) ** -0.5, 0.046875, ((0, 32),), jnp.float32),
        "self_lesser": centred(key_list[2], (WINDOW, 2, SITES, SITES), (SITES * WINDOW) ** -0.5, 0.046875, ((0, 32),), jnp.float32),
        "row_old": centred(key_list[3], (PAIRS, 2, 2, SITES, SITES), 1.0, 6.0, ((0, 32), (3, 8)), jnp.float32),
        "hopping": centred(key_list[4], (2, SITES, SITES), SITES ** -0.5, 0.375, (), jnp.float32),
        "damping": jnp.clip(jnp.exp(jax.random.uniform(key_list[5], (SITES,), jnp.float32, math.log(0.2), math.log(2.0))), 0.2, 2.0),
    }


step_size = 0.5
coupling_sq = 0.25


def contract(left, right, form):
    return jnp.einsum(form, left, right, precision=lax.Precision.HIGHEST)


def slot_plan(row_index, pair, half_block, blocks, window):
    positions = jnp.arange(2 * half_block, dtype=jnp.int32)
    times = jnp.where(positions < half_block, row_index * half_block + positions, (blocks - 1 - row_index) * half_block + positions - half_block)
    low_count = jnp.sum((times <= pair).astype(jnp.int32))
    slots = jnp.arange(2 * half_block + 1, dtype=jnp.int32)
    upper = slots - low_count
    picked = jnp.clip(jnp.where(slots < low_count, slots, upper), 0, 2 * half_block - 1)
    chosen = jnp.take(times, picked)
    weight_low = (slots < low_count).astype(jnp.float32)
    weight_high = ((slots >= low_count) & (upper < 2 * half_block) & (chosen <= window - 1 - pair)).astype(jnp.float32)
    return picked, chosen, weight_low, weight_high


def slot_terms(greater, lesser, tiles):
    g_re, g_im = greater[:, 0], greater[:, 1]
    t_re, t_im = tiles[:, 0], tiles[:, 1]
    l_re, l_im = lesser[:, 0], lesser[:, 1]
    direct_re = contract(g_re, t_re, "sij,sjk->sik") - contract(g_im, t_im, "sij,sjk->sik")
    direct_im = contract(g_re, t_im, "sij,sjk->sik") + contract(g_im, t_re, "sij,sjk->sik")
    mirror_re = contract(t_re, l_re, "sji,sjk->sik") + contract(t_im, l_im, "sji,sjk->sik")
    mirror_im = contract(t_re, l_im, "sji,sjk->sik") - contract(t_im, l_re, "sji,sjk->sik")
    return jnp.stack([direct_re - mirror_re, direct_im - mirror_im], axis=1)


def split_terms(terms, weight_low, weight_high):
    low = contract(weight_low, terms, "s,sxik->xik")
    high = contract(weight_high, terms, "s,sxik->xik")
    return jnp.stack([low, high])


def update(row_old, collision, hopping, damping):
    old_re, old_im = row_old[:, :, 0], row_old[:, :, 1]
    prod_re = contract(old_re, hopping[0], "pwik,kj->pwij") - contract(old_im, hopping[1], "pwik,kj->pwij")
    prod_im = contract(old_re, hopping[1], "pwik,kj->pwij") + contract(old_im, hopping[0], "pwik,kj->pwij")
    scale = 1.0 / (1.0 + step_size * damping)
    new_re = (old_re + step_size * (prod_im + collision[:, :, 0])) * scale
    new_im = (old_im + step_size * (collision[:, :, 1] - prod_re)) * scale
    return jnp.stack([new_re, new_im], axis=2)


def cubic(row_new, hopping):
    a_re, a_im = row_new[:, :, 0], row_new[:, :, 1]
    magnitude = a_re * a_re + a_im * a_im
    sig_re = -coupling_sq * magnitude * a_re
    sig_im = -coupling_sq * magnitude * a_im
    out_re = contract(sig_re, hopping[0], "pwik,kj->pwij") - contract(sig_im, hopping[1], "pwik,kj->pwij")
    out_im = contract(sig_re, hopping[1], "pwik,kj->pwij") + contract(sig_im, hopping[0], "pwik,kj->pwij")
    return jnp.stack([out_re, out_im], axis=2)


def reference(hist_lesser, self_greater, self_lesser, row_old, hopping, damping):
    sites = hist_lesser.shape[4]

    def pair_column(pair):
        def add_row(row_index, total):
            picked, chosen, weight_low, weight_high = slot_plan(row_index, pair, HALF_BLOCK, 2 * N_TROW, WINDOW)
            block = lax.dynamic_index_in_dim(hist_lesser, row_index, 0, False)
            tiles = lax.dynamic_index_in_dim(block, pair, 0, False)
            greater = jnp.take(self_greater, chosen, axis=0)
            lesser = jnp.take(self_lesser, chosen, axis=0)
            return total + split_terms(slot_terms(greater, lesser, tiles), weight_low, weight_high)

        return lax.fori_loop(0, N_TROW, add_row, jnp.zeros((2, 2, sites, sites), jnp.float32))

    collision = lax.map(pair_column, jnp.arange(PAIRS, dtype=jnp.int32))
    row_new = update(row_old, collision, hopping, damping)
    return row_new, cubic(row_new, hopping)
```

```python
import functools

import jax
import jax.numpy as jnp
from jax import lax
from jax.experimental import pallas as pl
from jax.experimental.pallas import tpu as pltpu
from jax.sharding import PartitionSpec as P

step_size = 0.5
coupling_sq = 0.25
MESH = pl.DeviceIdType.MESH
F32 = jnp.float32
BF16 = jnp.bfloat16
N = 256


def split(value):
    hi = value.astype(BF16)
    return hi, (value - hi.astype(F32)).astype(BF16)


def dot(a, b):
    return jnp.dot(a, b, preferred_element_type=F32)


def kernel(hist, sg, sl, old_ref, hop_ref, damp_ref, new_ref, out_ref,
           tiles, buf, gl, rg, sgl, slr, hop, acc, pbuf, xbuf, zbuf,
           tile_sem, own_sem, sc_send, sc_recv, g_send, g_recv, x_send, x_recv, z_send, z_recv):
    r = lax.axis_index("trow")
    k = lax.axis_index("tcol")
    z, g = r // 2, r % 2
    zh, y, x = k // 16, (k // 4) % 4, k % 4

    def dev(zz, gg, zzh, yy, xx):
        return (zz * 2 + gg, zzh * 16 + yy * 4 + xx)

    def place(half, zz, gg):
        ys = jnp.where(half == 0, zz, 3 - zz)
        xb = jnp.where(half == 0, 2 * gg, 2 - 2 * gg)
        return ys, xb

    near_half, far_half = zh, 1 - zh
    low_count = jnp.clip(k - 4 * r + 1, 0, 4)
    high_count = jnp.clip(4 + 4 * r - k, 0, 4)

    def tile_copy(t):
        return pltpu.make_async_copy(hist.at[0, 0, t], tiles.at[t], tile_sem.at[t])

    for t in range(9):
        tile_copy(t).start()

    sigma = x % 2
    my_group = jnp.where(zh == 0, x // 2, 1 - x // 2)
    near_row, near_base = place(near_half, z, g)
    far_row, far_base = place(far_half, z, g)
    near_source = (y == near_row) & (g == my_group)
    far_target = jnp.where(zh == 0, y, 3 - y)
    far_source = (g == my_group) & (((z == 3) & (far_target < 2)) | ((z == 0) & (far_target >= 2)))

    def residence(base, row):
        xr = (x - base + 4) % 4
        sig = jnp.where((xr == 1) | (xr == 2), 1, 0)
        return (y - row + 4) % 4, jnp.where(xr >= 2, 1, 0), base + sig

    near_y, near_e, near_x = residence(near_base, near_row)
    far_y, far_e, far_x = residence(far_base, far_row)
    self_block = (near_y == 0) & (near_e == 0)

    barrier = pltpu.get_barrier_semaphore()

    def greet(d):
        pl.semaphore_signal(barrier, inc=1, device_id=d, device_id_type=MESH)

    for s in (1, 3):
        greet(dev(z, g, zh, y, (x + s) % 4))
        greet(dev(z, g, zh, (y + s) % 4, x))
    greet(dev(z, 1 - g, zh, y, x))
    for s in (1, 2, 3):
        greet(dev((z + s) % 4, g, zh, y, x))

    @pl.when(jnp.logical_not(self_block))
    def _():
        greet(dev(z, g, zh, near_row, near_x))

    greet(dev(jnp.where(z < 2, 3, 0), g, 1 - zh, far_row, far_x))
    pl.semaphore_wait(barrier, 8 + 7 * near_source.astype(jnp.int32) + 8 * far_source.astype(jnp.int32))

    def scatter_copy(f, yr, e):
        src = (sg if yr < 2 else sl).at[e, yr % 2]
        row = y
        dy, dx = (row + yr) % 4, (x + e * (2 * sigma - 1) + 4) % 4
        to = dev(z, g, zh, dy, dx) if f == 0 else dev(far_target, g, 1 - zh, dy, dx)
        return pltpu.make_async_remote_copy(
            src_ref=src, dst_ref=buf.at[f, 4 * dy + dx], send_sem=sc_send.at[f, yr, e], recv_sem=sc_recv.at[f],
            device_id=to, device_id_type=MESH)

    def own_copy():
        return pltpu.make_async_copy(sg.at[0, 0], buf.at[0, 4 * y + x], own_sem.at[0])

    order = [(yr, e) for yr in (1, 3, 2, 0) for e in (0, 1)]

    @pl.when(near_source)
    def _():
        own_copy().start()
        for yr, e in order:
            if (yr, e) != (0, 0):
                scatter_copy(0, yr, e).start()

    @pl.when(far_source)
    def _():
        for yr, e in order:
            scatter_copy(1, yr, e).start()

    def wait_own(f):
        slot = 4 * y + x
        got = pltpu.make_async_remote_copy(
            src_ref=buf.at[f, slot], dst_ref=buf.at[f, slot], send_sem=sc_send.at[f, 0, 0], recv_sem=sc_recv.at[f],
            device_id=dev(z, 1 - g, zh, y, x), device_id_type=MESH)
        if f == 1:
            got.wait_recv()
        else:
            @pl.when(self_block)
            def _():
                own_copy().wait()

            @pl.when(jnp.logical_not(self_block))
            def _():
                got.wait_recv()

    def block(h, dp, dq):
        if h == 0:
            return 4 * ((y + dq + 4) % 4) + (x + dp + 4) % 4
        return 4 * ((y + dp + 4) % 4) + (x + dq + 4) % 4

    def hop_copy(f, h, e, way, fwd, at):
        sign = 1 if way == 0 else -1
        back = -sign * (fwd + at)
        dp, dq = (back, 0) if e == 0 else (e - 1, back)
        rows = pl.ds(h * 128 + way * 64, 64) if fwd else pl.ds(h * 128, 128)
        ref = buf.at[f, block(h, dp, dq), rows]
        along_x = (h == 0) == (e == 0)
        to = dev(z, g, zh, y, (x + sign + 4) % 4) if along_x else dev(z, g, zh, (y + sign + 4) % 4, x)
        return pltpu.make_async_remote_copy(
            src_ref=ref, dst_ref=ref, send_sem=g_send.at[f, h, e, way, fwd], recv_sem=g_recv.at[f, h, e, way, fwd],
            device_id=to, device_id_type=MESH)

    def send(f, h, e, way, fwd):
        hop_copy(f, h, e, way, fwd, 0).start()

    def recv(f, h, e, way, fwd):
        hop_copy(f, h, e, way, fwd, 1).wait_recv()

    def step_own(f):
        wait_own(f)
        for e in (0, 1):
            for h in (0, 1):
                for way in (0, 1):
                    send(f, h, e, way, 0)

    def step_first(f):
        for h in (0, 1):
            for way in (0, 1):
                recv(f, h, 0, way, 0)
                send(f, h, 0, way, 1)
        for way in (0, 1):
            for h in (0, 1):
                for w2 in (0, 1):
                    send(f, h, 4 if way == 0 else 2, w2, 0)

    def step_first_far(f):
        for h in (0, 1):
            for way in (0, 1):
                recv(f, h, 0, way, 1)
            for w2 in (0, 1):
                send(f, h, 3, w2, 0)

    def step_second(f, e):
        for h in (0, 1):
            for way in (0, 1):
                recv(f, h, e, way, 0)
                send(f, h, e, way, 1)

    def step_last(f, h, e):
        for way in (0, 1):
            recv(f, h, e, way, 1)

    def prepare_tile(t):
        tile_copy(t).wait()
        for part in (0, 1):
            value = tiles[t, part]
            for level, piece in enumerate(split(value)):
                gl[t, level, :, part * N:(part + 1) * N] = piece.T
                if part == 0:
                    rg[t, level, :N, :N] = piece
                    rg[t, level, N:, N:] = piece
                else:
                    rg[t, level, N:, :N] = -piece
                    rg[t, level, :N, N:] = piece

    def work(f, d):
        half = jnp.where(f == 0, near_half, far_half)
        row, base = (near_row, near_base) if f == 0 else (far_row, far_base)
        col = (x + d) % 4
        xr = (col - base + 4) % 4
        j = jnp.where(xr == 0, 0, jnp.where(xr == 3, 1, jnp.where(xr == 1, 2, 3)))
        low = half == 0

        def product(t, u):
            total = dot(sgl[0], rg[t, 0]) + dot(gl[t, 0], slr[0])
            total += dot(sgl[0], rg[t, 1]) + dot(gl[t, 0], slr[1])
            total += dot(sgl[1], rg[t, 0]) + dot(gl[t, 1], slr[0])
            acc[u] += total.reshape(4, 2, 32, 2 * N)

        @pl.when(low | (j < high_count))
        def _():
            for i in range(4):
                value = buf[f, 4 * ((row + i) % 4) + col]
                for level, piece in enumerate(split(value)):
                    if i < 2:
                        sgl[level, :, i * N:(i + 1) * N] = piece
                    elif i == 2:
                        slr[level, :N, :N] = -piece
                        slr[level, N:, N:] = piece
                    else:
                        slr[level, N:, :N] = -piece
                        slr[level, :N, N:] = -piece
            product(low_count + j + jnp.where(low, 0, 4), 1)

            @pl.when(low & (j < low_count))
            def _():
                product(j, 0)

    step_own(0)
    acc[...] = jnp.zeros_like(acc)
    for t in range(2):
        prepare_tile(t)
    step_first(0)
    for t in range(2, 4):
        prepare_tile(t)
    step_first_far(0)
    step_second(0, 1)
    for t in range(4, 6):
        prepare_tile(t)
    step_second(0, 2)
    step_second(0, 4)
    step_own(1)
    for t in range(6, 8):
        prepare_tile(t)
    step_second(0, 3)
    step_first(1)
    prepare_tile(8)
    step_last(0, 0, 1)
    work(0, 0)
    step_first_far(1)
    step_last(0, 0, 2)
    work(0, 1)
    step_second(1, 1)
    step_last(0, 0, 4)
    work(0, 3)
    step_second(1, 2)
    step_second(1, 4)
    step_last(0, 0, 3)
    for e in range(1, 5):
        step_last(0, 1, e)
    work(0, 2)
    step_second(1, 3)
    step_last(1, 0, 1)
    work(1, 0)
    step_last(1, 0, 2)
    work(1, 1)
    step_last(1, 0, 4)
    work(1, 3)

    for part in (0, 1):
        for level, piece in enumerate(split(hop_ref[part])):
            if part == 0:
                hop[level, :N, :N] = piece
                hop[level, N:, N:] = piece
            else:
                hop[level, N:, :N] = -piece
                hop[level, :N, N:] = piece

    def hopped(value):
        hi, lo = split(value)
        return dot(hi, hop[0]) + dot(hi, hop[1]) + dot(lo, hop[0])

    old_re = jnp.concatenate([old_ref[0, 0, 0], old_ref[0, 1, 0]], axis=0)
    old_im = jnp.concatenate([old_ref[0, 0, 1], old_ref[0, 1, 1]], axis=0)
    prod = hopped(jnp.concatenate([old_re, old_im], axis=1))

    step_last(1, 0, 3)
    for e in range(1, 5):
        step_last(1, 1, e)
    work(1, 2)

    def pair_copy(u):
        return pltpu.make_async_remote_copy(
            src_ref=acc.at[u, :, 1 - g], dst_ref=xbuf.at[u], send_sem=x_send.at[u], recv_sem=x_recv.at[u],
            device_id=dev(z, 1 - g, zh, y, x), device_id_type=MESH)

    def line_copy(u, s, at):
        to = (z + s) % 4
        slot = z if at == 0 else (z - s + 4) % 4
        return pltpu.make_async_remote_copy(
            src_ref=pbuf.at[u, to], dst_ref=zbuf.at[u, slot], send_sem=z_send.at[u, s], recv_sem=z_recv.at[u, s],
            device_id=dev(to, g, zh, y, x), device_id_type=MESH)

    for u in (0, 1):
        pair_copy(u).start()
    for u in (0, 1):
        pair_copy(u).wait_recv()
        pbuf[u] = acc[u, :, g] + xbuf[u]
        for s in (1, 2, 3):
            line_copy(u, s, 0).start()
    sums = []
    for u in (0, 1):
        total = pbuf[u, z]
        for s in (1, 2, 3):
            line_copy(u, s, 1).wait_recv()
            total = total + zbuf[u, (z - s + 4) % 4]
        sums.append(total)
    col = jnp.concatenate(sums, axis=0)

    scale = 1.0 / (1.0 + step_size * damp_ref[...])
    new_re = (old_re + step_size * (prod[:, N:] + col[:, :N])) * scale
    new_im = (old_im + step_size * (col[:, N:] - prod[:, :N])) * scale
    for u in (0, 1):
        new_ref[0, u, 0] = new_re[32 * u:32 * u + 32]
        new_ref[0, u, 1] = new_im[32 * u:32 * u + 32]
    magnitude = -coupling_sq * (new_re * new_re + new_im * new_im)
    sig = hopped(jnp.concatenate([magnitude * new_re, magnitude * new_im], axis=1))
    for u in (0, 1):
        out_ref[0, u, 0] = sig[32 * u:32 * u + 32, :N]
        out_ref[0, u, 1] = sig[32 * u:32 * u + 32, N:]

    @pl.when(near_source)
    def _():
        for yr, e in order:
            if (yr, e) != (0, 0):
                scatter_copy(0, yr, e).wait_send()

    @pl.when(far_source)
    def _():
        for yr, e in order:
            scatter_copy(1, yr, e).wait_send()

    for f in (0, 1):
        for h in (0, 1):
            for e in range(5):
                for way in (0, 1):
                    for fwd in (0, 1):
                        hop_copy(f, h, e, way, fwd, 0).wait_send()
    for u in (0, 1):
        pair_copy(u).wait_send()
        for s in (1, 2, 3):
            line_copy(u, s, 0).wait_send()


def on_device(hist, sg, sl, row_old, hopping, damping):
    any_space = pl.BlockSpec(memory_space=pl.ANY)
    vmem = pl.BlockSpec(memory_space=pltpu.VMEM)
    dma = pltpu.SemaphoreType.DMA
    shape = jax.ShapeDtypeStruct((1, 2, 2, 32, N), F32)
    return tuple(pl.pallas_call(
        kernel,
        out_shape=(shape, shape),
        in_specs=[any_space, any_space, any_space, vmem, vmem, vmem],
        out_specs=(vmem, vmem),
        scratch_shapes=[
            pltpu.VMEM((9, 2, N, N), F32),
            pltpu.VMEM((2, 16, N, N), F32),
            pltpu.VMEM((9, 2, N, 2 * N), BF16),
            pltpu.VMEM((9, 2, 2 * N, 2 * N), BF16),
            pltpu.VMEM((2, N, 2 * N), BF16),
            pltpu.VMEM((2, 2 * N, 2 * N), BF16),
            pltpu.VMEM((2, 2 * N, 2 * N), BF16),
            pltpu.VMEM((2, 4, 2, 32, 2 * N), F32),
            pltpu.VMEM((2, 4, 32, 2 * N), F32),
            pltpu.VMEM((2, 4, 32, 2 * N), F32),
            pltpu.VMEM((2, 4, 32, 2 * N), F32),
            dma((9,)), dma((1,)), dma((2, 4, 2)), dma((2,)), dma((2, 2, 5, 2, 2)), dma((2, 2, 5, 2, 2)),
            dma((2,)), dma((2,)), dma((2, 4)), dma((2, 4)),
        ],
        compiler_params=pltpu.CompilerParams(collective_id=0, has_side_effects=True, vmem_limit_bytes=56 << 20),
        cost_estimate=pl.CostEstimate(flops=7 * 10**9, bytes_accessed=10**7, transcendentals=0),
        name="collide",
    )(hist, sg, sl, row_old, hopping, damping.reshape(1, N)))


def solution(mesh):
    in_specs = (
        P("trow", "tcol", None, None, None, None),
        P("tcol", None, None, None),
        P("tcol", None, None, None),
        P("tcol", None, None, "trow", None),
        P(),
        P(),
    )
    out_specs = (P("tcol", None, None, "trow", None), P("tcol", None, None, "trow", None))
    return jax.shard_map(on_device, mesh=mesh, in_specs=in_specs, out_specs=out_specs, check_vma=False)
```

```python
import functools

import jax
import jax.numpy as jnp
from jax import lax
from jax.experimental import pallas as pl
from jax.experimental.pallas import tpu as pltpu
from jax.sharding import PartitionSpec as P

step_size = 0.5
coupling_sq = 0.25
MESH = pl.DeviceIdType.MESH
F32 = jnp.float32
BF16 = jnp.bfloat16
N = 256


def split(value):
    hi = value.astype(BF16)
    return hi, (value - hi.astype(F32)).astype(BF16)


def dot(a, b):
    return jnp.dot(a, b, preferred_element_type=F32)


def kernel(hist, sg, sl, old_any, hop_any, damp_any, new_ref, out_ref,
           old_ref, hop_ref, damp_ref, small_sem, tiles, buf, gl, rg, sgl, slr, hop, prod, acc, pbuf, xbuf, zbuf,
           tile_sem, own_sem, sc_send, far_send, far_recv, sc_recv, g_send, g_recv, x_send, x_recv, z_send, z_recv):
    r = lax.axis_index("trow")
    k = lax.axis_index("tcol")
    z, g = r // 2, r % 2
    zh, y, x = k // 16, (k // 4) % 4, k % 4

    def dev(zz, gg, zzh, yy, xx):
        return (zz * 2 + gg, zzh * 16 + yy * 4 + xx)

    def place(half, zz, gg):
        ys = jnp.where(half == 0, zz, 3 - zz)
        xb = jnp.where(half == 0, 2 * gg, 2 - 2 * gg)
        return ys, xb

    low_count = jnp.clip(k - 4 * r + 1, 0, 4)
    high_count = jnp.clip(4 + 4 * r - k, 0, 4)

    def tile_copy(t):
        return pltpu.make_async_copy(hist.at[0, 0, t], tiles.at[t], tile_sem.at[t])

    sigma = x % 2
    my_group = jnp.where(zh == 0, x // 2, 1 - x // 2)
    near_row, near_base = place(zh, z, g)
    near_source = (y == near_row) & (g == my_group)
    xr = (x - near_base + 4) % 4
    near_x = near_base + jnp.where((xr == 1) | (xr == 2), 1, 0)
    self_block = (y == near_row) & (xr < 2)
    slot = 4 * y + x

    barrier = pltpu.get_barrier_semaphore()

    def greet(d):
        pl.semaphore_signal(barrier, inc=1, device_id=d, device_id_type=MESH)

    greet(dev(z, g, 1 - zh, y, x))

    @pl.when(jnp.logical_not(self_block))
    def _():
        greet(dev(z, g, zh, near_row, near_x))

    for s in (2, 1, 3):
        greet(dev((z + s) % 4, g, zh, y, x))
    for s in (1, 3):
        greet(dev(z, g, zh, y, (x + s) % 4))
        greet(dev(z, g, zh, (y + s) % 4, x))
    greet(dev(z, 1 - g, zh, y, x))
    pl.semaphore_wait(barrier, 9 + 7 * near_source.astype(jnp.int32))

    small = [pltpu.make_async_copy(src, dst, small_sem.at[i]) for i, (src, dst) in enumerate(
        ((old_any, old_ref), (hop_any, hop_ref), (damp_any, damp_ref)))]

    def piece_of(ref, h):
        return ref.at[pl.ds(h * 128, 128)]

    def scatter_copy(yr, e, h):
        src = (sg if yr < 2 else sl).at[e, yr % 2]
        dy, dx = (y + yr) % 4, (x + e * (2 * sigma - 1) + 4) % 4
        return pltpu.make_async_remote_copy(
            src_ref=piece_of(src, h), dst_ref=piece_of(buf.at[zh, 4 * dy + dx], h),
            send_sem=sc_send.at[yr, e, h], recv_sem=sc_recv.at[h], device_id=dev(z, g, zh, dy, dx), device_id_type=MESH)

    def own_copy(h):
        return pltpu.make_async_copy(piece_of(sg.at[0, 0], h), piece_of(buf.at[zh, slot], h), own_sem.at[h])

    def far_copy(half, h):
        ref = piece_of(buf.at[half, slot], h)
        return pltpu.make_async_remote_copy(
            src_ref=ref, dst_ref=ref, send_sem=far_send.at[h], recv_sem=far_recv.at[h],
            device_id=dev(z, g, 1 - zh, y, x), device_id_type=MESH)

    order = [(yr, e) for yr in (2, 1, 3, 0) for e in (1, 0) if (yr, e) != (0, 0)]

    @pl.when(near_source)
    def _():
        for h in (0, 1):
            own_copy(h).start()
            for yr, e in order:
                scatter_copy(yr, e, h).start()

    for t in range(9):
        tile_copy(t).start()
    for copy in small:
        copy.start()

    def wait_own(f, h):
        @pl.when(self_block & (zh == f))
        def _():
            own_copy(h).wait()

        @pl.when(jnp.logical_not(self_block) & (zh == f))
        def _():
            ref = piece_of(buf.at[f, slot], h)
            pltpu.make_async_remote_copy(
                src_ref=ref, dst_ref=ref, send_sem=sc_send.at[0, 0, h], recv_sem=sc_recv.at[h],
                device_id=dev(z, 1 - g, zh, y, x), device_id_type=MESH).wait_recv()

        @pl.when(zh == f)
        def _():
            far_copy(f, h).start()

        @pl.when(zh != f)
        def _():
            far_copy(f, h).wait_recv()

    def block(h, dp, dq):
        if h == 0:
            return 4 * ((y + dq + 4) % 4) + (x + dp + 4) % 4
        return 4 * ((y + dp + 4) % 4) + (x + dq + 4) % 4

    def hop_copy(f, h, e, way, fwd, at):
        sign = 1 if way == 0 else -1
        back = -sign * (fwd + at)
        dp, dq = (back, 0) if e == 0 else (e - 1, back)
        rows = pl.ds(h * 128 + way * 64, 64) if fwd else pl.ds(h * 128, 128)
        ref = buf.at[f, block(h, dp, dq), rows]
        along_x = (h == 0) == (e == 0)
        to = dev(z, g, zh, y, (x + sign + 4) % 4) if along_x else dev(z, g, zh, (y + sign + 4) % 4, x)
        return pltpu.make_async_remote_copy(
            src_ref=ref, dst_ref=ref, send_sem=g_send.at[f, h, e, way, fwd], recv_sem=g_recv.at[f, h, e, way, fwd],
            device_id=to, device_id_type=MESH)

    def send(f, h, e, way, fwd):
        hop_copy(f, h, e, way, fwd, 0).start()

    def recv(f, h, e, way, fwd):
        hop_copy(f, h, e, way, fwd, 1).wait_recv()

    need_high = (zh == 0) | (z >= 2)

    def step(fn):
        def run(f, *args):
            if f == 0:
                fn(f, *args)
            else:
                @pl.when(need_high)
                def _():
                    fn(f, *args)
        return run

    def step_own(f):
        for h in (0, 1):
            wait_own(f, h)

            @step
            def first_sends(f):
                for e in (0, 1) if f == 0 else (0,):
                    for way in (0, 1):
                        send(f, h, e, way, 0)
            first_sends(f)

    @step
    def push(f, *stages):
        for e in stages:
            for h in (0, 1):
                for way in (0, 1):
                    send(f, h, e, way, 0)

    @step
    def step_first(f):
        for h in (0, 1):
            for way in (0, 1):
                recv(f, h, 0, way, 0)
                send(f, h, 0, way, 1)
            if f == 0:
                for e in (2, 4):
                    for way in (0, 1):
                        send(f, h, e, way, 0)

    @step
    def step_first_far(f):
        for h in (0, 1):
            for way in (0, 1):
                recv(f, h, 0, way, 1)
            if f == 0:
                for way in (0, 1):
                    send(f, h, 3, way, 0)

    @step
    def step_second(f, e):
        for h in (0, 1):
            for way in (0, 1):
                recv(f, h, e, way, 0)
                send(f, h, e, way, 1)

    @step
    def step_last(f, h, e):
        for way in (0, 1):
            recv(f, h, e, way, 1)

    def prepare_tile(t):
        tile_copy(t).wait()
        for part in (0, 1):
            value = tiles[t, part]
            for level, piece in enumerate(split(value)):
                gl[t, level, :, part * N:(part + 1) * N] = piece.T
                if part == 0:
                    rg[t, level, :N, :N] = piece
                    rg[t, level, N:, N:] = piece
                else:
                    rg[t, level, N:, :N] = -piece
                    rg[t, level, :N, N:] = piece

    def work(f, d):
        row, base = place(f, z, g)
        col = (x + d) % 4
        xr = (col - base + 4) % 4
        j = jnp.where(xr == 0, 0, jnp.where(xr == 3, 1, jnp.where(xr == 1, 2, 3)))

        def product(t, u):
            total = dot(sgl[0], rg[t, 0]) + dot(gl[t, 0], slr[0])
            total += dot(sgl[0], rg[t, 1]) + dot(gl[t, 0], slr[1])
            total += dot(sgl[1], rg[t, 0]) + dot(gl[t, 1], slr[0])
            acc[u] += total.reshape(4, 2, 32, 2 * N)

        def both():
            for i in range(4):
                value = buf[f, 4 * ((row + i) % 4) + col]
                for level, piece in enumerate(split(value)):
                    if i < 2:
                        sgl[level, :, i * N:(i + 1) * N] = piece
                    elif i == 2:
                        slr[level, :N, :N] = -piece
                        slr[level, N:, N:] = piece
                    else:
                        slr[level, N:, :N] = -piece
                        slr[level, :N, N:] = -piece
            product(low_count + j + 4 * f, 1)
            if f == 0:
                @pl.when(j < low_count)
                def _():
                    product(j, 0)

        if f == 0:
            both()
        else:
            pl.when(j < high_count)(both)

    def pair_copy(u):
        return pltpu.make_async_remote_copy(
            src_ref=acc.at[u, :, 1 - g], dst_ref=xbuf.at[u], send_sem=x_send.at[u], recv_sem=x_recv.at[u],
            device_id=dev(z, 1 - g, zh, y, x), device_id_type=MESH)

    def line_copy(u, s, at):
        to = (z + s) % 4
        place_of = z if at == 0 else (z - s + 4) % 4
        return pltpu.make_async_remote_copy(
            src_ref=pbuf.at[u, to], dst_ref=zbuf.at[u, place_of], send_sem=z_send.at[u, s], recv_sem=z_recv.at[u, s],
            device_id=dev(to, g, zh, y, x), device_id_type=MESH)

    def sum_pair(u):
        pair_copy(u).wait_recv()
        pbuf[u] = acc[u, :, g] + xbuf[u]
        for s in (1, 2, 3):
            line_copy(u, s, 0).start()

    def prepare_hop():
        for part in (0, 1):
            for level, piece in enumerate(split(hop_ref[part])):
                if part == 0:
                    hop[level, :N, :N] = piece
                    hop[level, N:, N:] = piece
                else:
                    hop[level, N:, :N] = -piece
                    hop[level, :N, N:] = piece

    def hopped(value):
        hi, lo = split(value)
        return dot(hi, hop[0]) + dot(hi, hop[1]) + dot(lo, hop[0])

    def multiply_old():
        for u in (0, 1):
            prod[u] = hopped(jnp.concatenate([old_ref[0, u, 0], old_ref[0, u, 1]], axis=1))

    def finish(u):
        col = pbuf[u, z]
        for s in (1, 2, 3):
            line_copy(u, s, 1).wait_recv()
            col = col + zbuf[u, (z - s + 4) % 4]
        scale = 1.0 / (1.0 + step_size * damp_ref[...])
        new_re = (old_ref[0, u, 0] + step_size * (prod[u, :, N:] + col[:, :N])) * scale
        new_im = (old_ref[0, u, 1] + step_size * (col[:, N:] - prod[u, :, :N])) * scale
        new_ref[0, u, 0] = new_re
        new_ref[0, u, 1] = new_im
        magnitude = -coupling_sq * (new_re * new_re + new_im * new_im)
        sig = hopped(jnp.concatenate([magnitude * new_re, magnitude * new_im], axis=1))
        out_ref[0, u, 0] = sig[:, :N]
        out_ref[0, u, 1] = sig[:, N:]

    def when_low_plane(*steps):
        @pl.when(zh == 0)
        def _():
            for fn, *args in steps:
                fn(*args)

    def when_high_plane(*steps):
        @pl.when(zh == 1)
        def _():
            for fn, *args in steps:
                fn(*args)

    acc[...] = jnp.zeros_like(acc)
    when_high_plane((step_own, 1), (step_first, 1), (step_first_far, 1))
    step_own(0)
    for t in range(2):
        prepare_tile(t)
    step_first(0)
    for t in range(2, 4):
        prepare_tile(t)
    step_first_far(0)
    step_second(0, 1)
    for t in range(4, 6):
        prepare_tile(t)
    step_second(0, 2)
    when_low_plane((step_own, 1))
    step_second(0, 4)
    for t in range(6, 9):
        prepare_tile(t)
    when_low_plane((step_first, 1))
    step_second(0, 3)
    when_low_plane((step_first_far, 1))
    push(1, 1, 2, 4, 3)
    for copy in small:
        copy.wait()
    prepare_hop()
    multiply_old()
    step_last(0, 0, 1)
    work(0, 0)
    step_last(0, 0, 2)
    work(0, 1)
    step_second(1, 1)
    step_last(0, 0, 4)
    work(0, 3)
    step_last(0, 0, 3)
    for e in range(1, 5):
        step_last(0, 1, e)
    work(0, 2)
    pair_copy(0).start()
    step_second(1, 2)
    sum_pair(0)
    step_second(1, 4)
    step_last(1, 0, 1)
    work(1, 0)
    finish(0)
    step_second(1, 3)
    step_last(1, 0, 2)
    work(1, 1)
    step_last(1, 0, 4)
    work(1, 3)
    step_last(1, 0, 3)
    for e in range(1, 5):
        step_last(1, 1, e)
    work(1, 2)
    pair_copy(1).start()
    sum_pair(1)
    finish(1)

    @pl.when(near_source)
    def _():
        for h in (0, 1):
            for yr, e in order:
                scatter_copy(yr, e, h).wait_send()

    for h in (0, 1):
        far_copy(zh, h).wait_send()
    @step
    def sends_left(f):
        for h in (0, 1):
            for e in range(5):
                for way in (0, 1):
                    for fwd in (0, 1):
                        hop_copy(f, h, e, way, fwd, 0).wait_send()

    sends_left(0)
    sends_left(1)
    for u in (0, 1):
        pair_copy(u).wait_send()
        for s in (1, 2, 3):
            line_copy(u, s, 0).wait_send()


def on_device(hist, sg, sl, row_old, hopping, damping):
    any_space = pl.BlockSpec(memory_space=pl.ANY)
    vmem = pl.BlockSpec(memory_space=pltpu.VMEM)
    dma = pltpu.SemaphoreType.DMA
    shape = jax.ShapeDtypeStruct((1, 2, 2, 32, N), F32)
    return tuple(pl.pallas_call(
        kernel,
        out_shape=(shape, shape),
        in_specs=[any_space] * 6,
        out_specs=(vmem, vmem),
        scratch_shapes=[
            pltpu.VMEM((1, 2, 2, 32, N), F32), pltpu.VMEM((2, N, N), F32), pltpu.VMEM((1, N), F32), dma((3,)),
            pltpu.VMEM((9, 2, N, N), F32),
            pltpu.VMEM((2, 16, N, N), F32),
            pltpu.VMEM((9, 2, N, 2 * N), BF16),
            pltpu.VMEM((9, 2, 2 * N, 2 * N), BF16),
            pltpu.VMEM((2, N, 2 * N), BF16),
            pltpu.VMEM((2, 2 * N, 2 * N), BF16),
            pltpu.VMEM((2, 2 * N, 2 * N), BF16),
            pltpu.VMEM((2, 32, 2 * N), F32),
            pltpu.VMEM((2, 4, 2, 32, 2 * N), F32),
            pltpu.VMEM((2, 4, 32, 2 * N), F32),
            pltpu.VMEM((2, 4, 32, 2 * N), F32),
            pltpu.VMEM((2, 4, 32, 2 * N), F32),
            dma((9,)), dma((2,)), dma((4, 2, 2)), dma((2,)), dma((2,)), dma((2,)), dma((2, 2, 5, 2, 2)), dma((2, 2, 5, 2, 2)),
            dma((2,)), dma((2,)), dma((2, 4)), dma((2, 4)),
        ],
        compiler_params=pltpu.CompilerParams(collective_id=0, has_side_effects=True, vmem_limit_bytes=56 << 20),
        cost_estimate=pl.CostEstimate(flops=7 * 10**9, bytes_accessed=10**7, transcendentals=0),
        name="collide",
    )(hist, sg, sl, row_old, hopping, damping.reshape(1, N)))


def solution(mesh):
    in_specs = (
        P("trow", "tcol", None, None, None, None),
        P("tcol", None, None, None),
        P("tcol", None, None, None),
        P("tcol", None, None, "trow", None),
        P(),
        P(),
    )
    out_specs = (P("tcol", None, None, "trow", None), P("tcol", None, None, "trow", None))
    return jax.shard_map(on_device, mesh=mesh, in_specs=in_specs, out_specs=out_specs, check_vma=False)
```

```python
import functools

import jax
import jax.numpy as jnp
from jax import lax
from jax.experimental import pallas as pl
from jax.experimental.pallas import tpu as pltpu
from jax.sharding import PartitionSpec as P

step_size = 0.5
coupling_sq = 0.25
MESH = pl.DeviceIdType.MESH
F32 = jnp.float32
BF16 = jnp.bfloat16
N = 256


def split(value):
    hi = value.astype(BF16)
    return hi, (value - hi.astype(F32)).astype(BF16)


def dot(a, b):
    return jnp.dot(a, b, preferred_element_type=F32)


def kernel(hist, sg, sl, old_any, hop_any, damp_any, new_ref, out_ref,
           old_ref, hop_ref, damp_ref, small_sem, tiles, buf, gl, rg, sgl, slr, hop, prod, acc, pbuf, xbuf, zbuf,
           tile_sem, own_sem, sc_send, far_send, far_recv, sc_recv, g_send, g_recv, x_send, x_recv, z_send, z_recv):
    r = lax.axis_index("trow")
    k = lax.axis_index("tcol")
    z, g = r // 2, r % 2
    zh, y, x = k // 16, (k // 4) % 4, k % 4

    def dev(zz, gg, zzh, yy, xx):
        return (zz * 2 + gg, zzh * 16 + yy * 4 + xx)

    def place(half, zz, gg):
        ys = jnp.where(half == 0, zz, 3 - zz)
        xb = jnp.where(half == 0, 2 * gg, 2 - 2 * gg)
        return ys, xb

    low_count = jnp.clip(k - 4 * r + 1, 0, 4)
    high_count = jnp.clip(4 + 4 * r - k, 0, 4)

    def tile_copy(t):
        return pltpu.make_async_copy(hist.at[0, 0, t], tiles.at[t], tile_sem.at[t])

    sigma = x % 2
    my_group = jnp.where(zh == 0, x // 2, 1 - x // 2)
    near_row, near_base = place(zh, z, g)
    near_source = (y == near_row) & (g == my_group)
    xr = (x - near_base + 4) % 4
    near_x = near_base + jnp.where((xr == 1) | (xr == 2), 1, 0)
    self_block = (y == near_row) & (xr < 2)
    slot = 4 * y + x

    barrier = pltpu.get_barrier_semaphore()

    def greet(d):
        pl.semaphore_signal(barrier, inc=1, device_id=d, device_id_type=MESH)

    greet(dev(z, g, 1 - zh, y, x))

    @pl.when(jnp.logical_not(self_block))
    def _():
        greet(dev(z, g, zh, near_row, near_x))

    for s in (2, 1, 3):
        greet(dev((z + s) % 4, g, zh, y, x))
    for s in (1, 3):
        greet(dev(z, g, zh, y, (x + s) % 4))
        greet(dev(z, g, zh, (y + s) % 4, x))
    greet(dev(z, 1 - g, zh, y, x))
    pl.semaphore_wait(barrier, 9 + 7 * near_source.astype(jnp.int32))

    small = [pltpu.make_async_copy(src, dst, small_sem.at[i]) for i, (src, dst) in enumerate(
        ((old_any, old_ref), (hop_any, hop_ref), (damp_any, damp_ref)))]

    def piece_of(ref, h):
        return ref.at[pl.ds(h * 128, 128)]

    def scatter_copy(yr, e, h):
        src = (sg if yr < 2 else sl).at[e, yr % 2]
        dy, dx = (y + yr) % 4, (x + e * (2 * sigma - 1) + 4) % 4
        return pltpu.make_async_remote_copy(
            src_ref=piece_of(src, h), dst_ref=piece_of(buf.at[zh, 4 * dy + dx], h),
            send_sem=sc_send.at[yr, e, h], recv_sem=sc_recv.at[h], device_id=dev(z, g, zh, dy, dx), device_id_type=MESH)

    def own_copy(h):
        return pltpu.make_async_copy(piece_of(sg.at[0, 0], h), piece_of(buf.at[zh, slot], h), own_sem.at[h])

    def far_copy(half, h):
        ref = piece_of(buf.at[half, slot], h)
        return pltpu.make_async_remote_copy(
            src_ref=ref, dst_ref=ref, send_sem=far_send.at[h], recv_sem=far_recv.at[h],
            device_id=dev(z, g, 1 - zh, y, x), device_id_type=MESH)

    order = [(yr, e) for yr in (2, 1, 3, 0) for e in (1, 0) if (yr, e) != (0, 0)]

    @pl.when(near_source)
    def _():
        for h in (0, 1):
            own_copy(h).start()
            for yr, e in order:
                scatter_copy(yr, e, h).start()

    for t in range(9):
        tile_copy(t).start()
    for copy in small:
        copy.start()

    def wait_own(f, h):
        @pl.when(self_block & (zh == f))
        def _():
            own_copy(h).wait()

        @pl.when(jnp.logical_not(self_block) & (zh == f))
        def _():
            ref = piece_of(buf.at[f, slot], h)
            pltpu.make_async_remote_copy(
                src_ref=ref, dst_ref=ref, send_sem=sc_send.at[0, 0, h], recv_sem=sc_recv.at[h],
                device_id=dev(z, 1 - g, zh, y, x), device_id_type=MESH).wait_recv()

        @pl.when(zh == f)
        def _():
            far_copy(f, h).start()

        @pl.when(zh != f)
        def _():
            far_copy(f, h).wait_recv()

    def block(h, dp, dq):
        if h == 0:
            return 4 * ((y + dq + 4) % 4) + (x + dp + 4) % 4
        return 4 * ((y + dp + 4) % 4) + (x + dq + 4) % 4

    def hop_copy(f, h, e, way, fwd, at):
        sign = 1 if way == 0 else -1
        back = -sign * (fwd + at)
        dp, dq = (back, 0) if e == 0 else (e - 1, back)
        rows = pl.ds(h * 128 + way * 64, 64) if fwd else pl.ds(h * 128, 128)
        ref = buf.at[f, block(h, dp, dq), rows]
        along_x = (h == 0) == (e == 0)
        to = dev(z, g, zh, y, (x + sign + 4) % 4) if along_x else dev(z, g, zh, (y + sign + 4) % 4, x)
        return pltpu.make_async_remote_copy(
            src_ref=ref, dst_ref=ref, send_sem=g_send.at[f, h, e, way, fwd], recv_sem=g_recv.at[f, h, e, way, fwd],
            device_id=to, device_id_type=MESH)

    def send(f, h, e, way, fwd):
        hop_copy(f, h, e, way, fwd, 0).start()

    def recv(f, h, e, way, fwd):
        hop_copy(f, h, e, way, fwd, 1).wait_recv()

    need_high = (zh == 0) | (z >= 2)

    def step(fn):
        def run(f, *args):
            if f == 0:
                fn(f, *args)
            else:
                @pl.when(need_high)
                def _():
                    fn(f, *args)
        return run

    def step_own(f):
        for h in (0, 1):
            wait_own(f, h)

            @step
            def first_sends(f):
                for e in (0, 1) if f == 0 else (0,):
                    for way in (0, 1):
                        send(f, h, e, way, 0)
            first_sends(f)

    @step
    def push(f, *stages):
        for e in stages:
            for h in (0, 1):
                for way in (0, 1):
                    send(f, h, e, way, 0)

    @step
    def step_first(f):
        for h in (0, 1):
            for way in (0, 1):
                recv(f, h, 0, way, 0)
                send(f, h, 0, way, 1)
            if f == 0:
                for e in (2, 4):
                    for way in (0, 1):
                        send(f, h, e, way, 0)

    @step
    def step_first_far(f):
        for h in (0, 1):
            for way in (0, 1):
                recv(f, h, 0, way, 1)
            if f == 0:
                for way in (0, 1):
                    send(f, h, 3, way, 0)

    @step
    def step_second(f, e):
        for h in (0, 1):
            for way in (0, 1):
                recv(f, h, e, way, 0)
                send(f, h, e, way, 1)

    @step
    def step_last(f, h, e):
        for way in (0, 1):
            recv(f, h, e, way, 1)

    def prepare_tile(t):
        tile_copy(t).wait()
        for part in (0, 1):
            value = tiles[t, part]
            for level, piece in enumerate(split(value)):
                gl[t, level, :, part * N:(part + 1) * N] = piece.T
                if part == 0:
                    rg[t, level, :N, :N] = piece
                    rg[t, level, N:, N:] = piece
                else:
                    rg[t, level, N:, :N] = -piece
                    rg[t, level, :N, N:] = piece

    def work(f, d):
        row, base = place(f, z, g)
        col = (x + d) % 4
        xr = (col - base + 4) % 4
        j = jnp.where(xr == 0, 0, jnp.where(xr == 3, 1, jnp.where(xr == 1, 2, 3)))

        def product(t, u):
            total = dot(sgl[0], rg[t, 0]) + dot(gl[t, 0], slr[0])
            total += dot(sgl[0], rg[t, 1]) + dot(gl[t, 0], slr[1])
            total += dot(sgl[1], rg[t, 0]) + dot(gl[t, 1], slr[0])
            acc[u] += total.reshape(4, 2, 32, 2 * N)

        def both():
            for i in range(4):
                value = buf[f, 4 * ((row + i) % 4) + col]
                for level, piece in enumerate(split(value)):
                    if i < 2:
                        sgl[level, :, i * N:(i + 1) * N] = piece
                    elif i == 2:
                        slr[level, :N, :N] = -piece
                        slr[level, N:, N:] = piece
                    else:
                        slr[level, N:, :N] = -piece
                        slr[level, :N, N:] = -piece
            product(low_count + j + 4 * f, 1)
            if f == 0:
                @pl.when(j < low_count)
                def _():
                    product(j, 0)

        if f == 0:
            both()
        else:
            pl.when(j < high_count)(both)

    def pair_copy(u):
        return pltpu.make_async_remote_copy(
            src_ref=acc.at[u, :, 1 - g], dst_ref=xbuf.at[u], send_sem=x_send.at[u], recv_sem=x_recv.at[u],
            device_id=dev(z, 1 - g, zh, y, x), device_id_type=MESH)

    def line_copy(u, s, at):
        to = (z + s) % 4
        place_of = z if at == 0 else (z - s + 4) % 4
        return pltpu.make_async_remote_copy(
            src_ref=pbuf.at[u, to], dst_ref=zbuf.at[u, place_of], send_sem=z_send.at[u, s], recv_sem=z_recv.at[u, s],
            device_id=dev(to, g, zh, y, x), device_id_type=MESH)

    def sum_pair(u):
        pair_copy(u).wait_recv()
        for s in (2, 1, 3, 0):
            to = (z + s) % 4
            pbuf[u, to] = acc[u, to, g] + xbuf[u, to]
            if s:
                line_copy(u, s, 0).start()

    def prepare_hop():
        for part in (0, 1):
            for level, piece in enumerate(split(hop_ref[part])):
                if part == 0:
                    hop[level, :N, :N] = piece
                    hop[level, N:, N:] = piece
                else:
                    hop[level, N:, :N] = -piece
                    hop[level, :N, N:] = piece

    def hopped(value):
        hi, lo = split(value)
        return dot(hi, hop[0]) + dot(hi, hop[1]) + dot(lo, hop[0])

    def multiply_old():
        for u in (0, 1):
            prod[u] = hopped(jnp.concatenate([old_ref[0, u, 0], old_ref[0, u, 1]], axis=1))

    def finish(u):
        col = pbuf[u, z]
        for s in (1, 2, 3):
            line_copy(u, s, 1).wait_recv()
            col = col + zbuf[u, (z - s + 4) % 4]
        scale = 1.0 / (1.0 + step_size * damp_ref[...])
        new_re = (old_ref[0, u, 0] + step_size * (prod[u, :, N:] + col[:, :N])) * scale
        new_im = (old_ref[0, u, 1] + step_size * (col[:, N:] - prod[u, :, :N])) * scale
        new_ref[0, u, 0] = new_re
        new_ref[0, u, 1] = new_im
        magnitude = -coupling_sq * (new_re * new_re + new_im * new_im)
        sig = hopped(jnp.concatenate([magnitude * new_re, magnitude * new_im], axis=1))
        out_ref[0, u, 0] = sig[:, :N]
        out_ref[0, u, 1] = sig[:, N:]

    def when_low_plane(*steps):
        @pl.when(zh == 0)
        def _():
            for fn, *args in steps:
                fn(*args)

    def when_high_plane(*steps):
        @pl.when(zh == 1)
        def _():
            for fn, *args in steps:
                fn(*args)

    acc[...] = jnp.zeros_like(acc)
    when_high_plane((step_own, 1), (step_first, 1), (step_first_far, 1))
    step_own(0)
    for t in range(2):
        prepare_tile(t)
    step_first(0)
    for t in range(2, 4):
        prepare_tile(t)
    step_first_far(0)
    step_second(0, 1)
    for t in range(4, 6):
        prepare_tile(t)
    step_second(0, 2)
    when_low_plane((step_own, 1))
    step_second(0, 4)
    for t in range(6, 9):
        prepare_tile(t)
    when_low_plane((step_first, 1))
    step_second(0, 3)
    when_low_plane((step_first_far, 1))
    push(1, 1, 2, 4, 3)
    for copy in small:
        copy.wait()
    prepare_hop()
    multiply_old()
    step_last(0, 0, 1)
    work(0, 0)
    step_last(0, 0, 2)
    work(0, 1)
    step_second(1, 1)
    step_last(0, 0, 4)
    work(0, 3)
    step_last(0, 0, 3)
    for e in range(1, 5):
        step_last(0, 1, e)
    work(0, 2)
    pair_copy(0).start()
    step_second(1, 2)
    sum_pair(0)
    step_second(1, 4)
    step_last(1, 0, 1)
    work(1, 0)
    finish(0)
    step_second(1, 3)
    step_last(1, 0, 2)
    work(1, 1)
    step_last(1, 0, 4)
    work(1, 3)
    step_last(1, 0, 3)
    for e in range(1, 5):
        step_last(1, 1, e)
    work(1, 2)
    pair_copy(1).start()
    sum_pair(1)
    finish(1)

    @pl.when(near_source)
    def _():
        for h in (0, 1):
            for yr, e in order:
                scatter_copy(yr, e, h).wait_send()

    for h in (0, 1):
        far_copy(zh, h).wait_send()
    @step
    def sends_left(f):
        for h in (0, 1):
            for e in range(5):
                for way in (0, 1):
                    for fwd in (0, 1):
                        hop_copy(f, h, e, way, fwd, 0).wait_send()

    sends_left(0)
    sends_left(1)
    for u in (0, 1):
        pair_copy(u).wait_send()
        for s in (1, 2, 3):
            line_copy(u, s, 0).wait_send()


def on_device(hist, sg, sl, row_old, hopping, damping):
    any_space = pl.BlockSpec(memory_space=pl.ANY)
    vmem = pl.BlockSpec(memory_space=pltpu.VMEM)
    dma = pltpu.SemaphoreType.DMA
    shape = jax.ShapeDtypeStruct((1, 2, 2, 32, N), F32)
    return tuple(pl.pallas_call(
        kernel,
        out_shape=(shape, shape),
        in_specs=[any_space] * 6,
        out_specs=(vmem, vmem),
        scratch_shapes=[
            pltpu.VMEM((1, 2, 2, 32, N), F32), pltpu.VMEM((2, N, N), F32), pltpu.VMEM((1, N), F32), dma((3,)),
            pltpu.VMEM((9, 2, N, N), F32),
            pltpu.VMEM((2, 16, N, N), F32),
            pltpu.VMEM((9, 2, N, 2 * N), BF16),
            pltpu.VMEM((9, 2, 2 * N, 2 * N), BF16),
            pltpu.VMEM((2, N, 2 * N), BF16),
            pltpu.VMEM((2, 2 * N, 2 * N), BF16),
            pltpu.VMEM((2, 2 * N, 2 * N), BF16),
            pltpu.VMEM((2, 32, 2 * N), F32),
            pltpu.VMEM((2, 4, 2, 32, 2 * N), F32),
            pltpu.VMEM((2, 4, 32, 2 * N), F32),
            pltpu.VMEM((2, 4, 32, 2 * N), F32),
            pltpu.VMEM((2, 4, 32, 2 * N), F32),
            dma((9,)), dma((2,)), dma((4, 2, 2)), dma((2,)), dma((2,)), dma((2,)), dma((2, 2, 5, 2, 2)), dma((2, 2, 5, 2, 2)),
            dma((2,)), dma((2,)), dma((2, 4)), dma((2, 4)),
        ],
        compiler_params=pltpu.CompilerParams(collective_id=0, has_side_effects=True, vmem_limit_bytes=56 << 20),
        cost_estimate=pl.CostEstimate(flops=7 * 10**9, bytes_accessed=10**7, transcendentals=0),
        name="collide",
    )(hist, sg, sl, row_old, hopping, damping.reshape(1, N)))


def solution(mesh):
    in_specs = (
        P("trow", "tcol", None, None, None, None),
        P("tcol", None, None, None),
        P("tcol", None, None, None),
        P("tcol", None, None, "trow", None),
        P(),
        P(),
    )
    out_specs = (P("tcol", None, None, "trow", None), P("tcol", None, None, "trow", None))
    return jax.shard_map(on_device, mesh=mesh, in_specs=in_specs, out_specs=out_specs, check_vma=False)
```
